32 devices in a mesh: req: 8 (over z, x), tp: 4 (over y, core).
Axes of the slice: x: 2, y: 2, z: 4, core: 2. Of those that a mesh axis runs over, the one named last changes fastest.
Arguments:
- residual: bfloat16 [768, 7168], P('req', 'tp'), may hold values from -3 to 3
- queries: bfloat16 [768, 7168], P('req', 'tp'), as said below
- fresh_token_keys: bfloat16 [768, 1024], P('req', 'tp'), may hold values from -6 to 6
- fresh_token_values: bfloat16 [768, 1024], P('req', 'tp'), may hold values from -6 to 6
- window_cache_keys: bfloat16 [48, 8, 768, 128], P('req', 'tp'), may hold values from -6 to 6
- window_cache_values: bfloat16 [48, 8, 768, 128], P('req', 'tp'), may hold values from -6 to 6
- rotated_sink_keys: bfloat16 [48, 8, 4, 128], P('req', 'tp'), may hold values from -9 to 9
- sink_value_rows: bfloat16 [48, 8, 4, 128], P('req', 'tp'), may hold values from -6 to 6
- slot_request: int32 [48], replicated, may hold values from 0 to 47, as said below
- cached_len: int32 [48], replicated, may hold values from 4 to 1539
- new_count: int32 [48], replicated, may hold values from 1 to 16, 576 in all
- out_weight: bfloat16 [7168, 7168], P('tp'), may hold values from -0.0625 to 0.0625
- norm_gain: bfloat16 [7168], P('tp'), may hold values from 0.5 to 1.5
- gate_weight: bfloat16 [7168, 20480], P('tp', 'req'), may hold values from -0.0625 to 0.0625
- up_weight: bfloat16 [7168, 20480], P('tp', 'req'), may hold values from -0.0625 to 0.0625
- down_weight: bfloat16 [20480, 7168], P('req', 'tp'), may hold values from -0.0390625 to 0.0390625
Outputs:
- block_output: bfloat16 [768, 7168], P('req', 'tp')
- decode_keys: bfloat16 [48, 8, 768, 128], P('req', 'tp')
- decode_values: bfloat16 [48, 8, 768, 128], P('req', 'tp')
The draws below stay inside these ranges and needn't reach their ends.
Inputs may be any that keep to these rules, and one draw needn't show every extreme that they name: `slot_request`: every request appears once; slot s belongs to group s // 6. Request r belongs to decode device r // 6, and the 6 requests of one group belong to 6 different decode devices. `queries`: query rows before rotation.
All inputs are finite; a program needn't handle non-finite values.
Results may differ from the reference program's by a relative error of at most 0.025.
Values may be sent and summed in bfloat16 or wider, within the bound.
A program may use at most 192 MiB of HBM per device.

```python
import math
import jax
import jax.numpy as jnp
import numpy as np
from jax import lax

D = 7168
QUERY_HEADS = 56
KEY_VALUE_HEADS = 8
HEAD_SIZE = 128
FF = 20480
RG = 6
NEW_TOKEN_SLOTS = 16
WINDOW_LENGTH = 768
SINK_POSITIONS = 4
REQUEST_COUNT = 48
TOKEN_SLOTS = 768
N_TP = 4


def draw_queries(key, part):
    values = jax.random.normal(key, (REQUEST_COUNT * NEW_TOKEN_SLOTS, QUERY_HEADS * HEAD_SIZE), jnp.float32) * 2.5
    return values.astype(jnp.bfloat16)


def draw_slot_request(key, part):
    groups = REQUEST_COUNT // RG
    key_one, key_two, key_three = jax.random.split(key, 3)
    anchor = jax.random.permutation(key_one, groups).astype(jnp.int32)
    shift_list = jax.random.permutation(key_two, groups).astype(jnp.int32)[:RG]
    scores = jax.random.randint(key_three, (groups, RG), 0, 1 << 20) * RG + jnp.arange(RG, dtype=jnp.int32)[None, :]
    inner_perm = jnp.argsort(scores, axis=1).astype(jnp.int32)
    block_ids = (anchor[:, None] + shift_list[None, :]) % groups
    within = inner_perm[block_ids, jnp.arange(RG, dtype=jnp.int32)[None, :]]
    return (block_ids * RG + within).reshape(REQUEST_COUNT).astype(jnp.int32)


def draw_cached_len(key, part):
    key_a, key_b, key_c, key_d = jax.random.split(key, 4)
    spread = jax.random.randint(key_a, (REQUEST_COUNT,), 0, 2 * WINDOW_LENGTH)
    halving = jax.random.randint(key_b, (REQUEST_COUNT,), 0, 4)
    values = SINK_POSITIONS + jnp.right_shift(spread, halving)
    longest = jax.random.randint(key_c, (), 0, REQUEST_COUNT)
    shortest = (longest + 1 + jax.random.randint(key_d, (), 0, REQUEST_COUNT - 1)) % REQUEST_COUNT
    values = values.at[longest].set(SINK_POSITIONS + 2 * WINDOW_LENGTH - 1).at[shortest].set(SINK_POSITIONS)
    return values.astype(jnp.int32)


def level_of(key, dims, shards, smallest, high):
    def one(axis_at, blocks):
        steps = jax.random.uniform(jax.random.fold_in(jax.random.fold_in(key, 6), axis_at), (blocks,), jnp.float32, smallest / len(shards), high / len(shards))
        return jnp.repeat(jnp.exp(steps), dims[axis_at] // blocks).reshape((-1,) + (1,) * (len(dims) - axis_at - 1))

    level = one(*shards[0])
    for cut in shards[1:]:
        level = level * one(*cut)
    return level


def length_profile(amount, total, bound, lean):
    loads = [(1 << 20) // math.isqrt(grade ** lean) + 1 for grade in range(2, amount + 1)]
    spare, given = total - bound - (amount - 1), [1] * (amount - 1)
    while spare > 0:
        movable = [i for i in range(amount - 1) if given[i] < bound]
        pool, budget = sum([loads[i] for i in movable]), spare
        for i in movable:
            extra = min(bound - given[i], max(1, budget * loads[i] // pool), spare)
            given[i] = given[i] + extra
            spare = spare - extra
    return np.array([bound] + given)


def uneven(own_key, count, total, most, slope):
    if count == 2:
        one = jax.random.randint(own_key, (), max(1, total - most), min(most, total - 1) + 1)
        return jnp.stack([one, total - one])
    sizes = jnp.asarray(length_profile(count, total, most, slope), jnp.int32)
    couples = (count - 1) // 2
    giver, sink = sizes[1:1 + 2 * couples:2], sizes[2:2 + 2 * couples:2]
    margin = jnp.minimum(giver - 1, most - sink)
    shifted = jax.random.randint(jax.random.fold_in(own_key, 1), (couples,), 0, 1 << 20) % (margin + 1)
    sizes = sizes.at[1:1 + 2 * couples:2].set(giver - shifted).at[2:2 + 2 * couples:2].set(sink + shifted)
    return sizes[jax.random.permutation(jax.random.fold_in(own_key, 2), count)]


def normal_values(rng, extent, deviation, most, pieces=(), kind=jnp.bfloat16):
    gain = level_of(rng, extent, pieces, -0.22, 0.18) if pieces else 1.0
    result = jax.random.normal(rng, extent, jnp.float32) * deviation * gain
    return jnp.minimum(jnp.maximum(result, -most), most).astype(kind)


def setup_inputs(seed: int = 0) -> dict:
    keys = jax.random.split(jax.random.key(seed), 17)
    residual = normal_values(keys[0], (TOKEN_SLOTS, D), 0.5, 3.0, ((0, 8), (1, 4)))
    queries = draw_queries(jax.random.fold_in(keys[16], 71), 0)
    fresh_token_keys = normal_values(keys[2], (TOKEN_SLOTS, KEY_VALUE_HEADS * HEAD_SIZE), 1.0, 6.0, ((0, 8), (1, 4)))
    fresh_token_values = normal_values(keys[3], (TOKEN_SLOTS, KEY_VALUE_HEADS * HEAD_SIZE), 1.0, 6.0, ((0, 8), (1, 4)))
    window_cache_keys = normal_values(keys[4], (REQUEST_COUNT, KEY_VALUE_HEADS, WINDOW_LENGTH, HEAD_SIZE), 1.0, 6.0, ((0, 8), (1, 4)))
    window_cache_values = normal_values(keys[5], (REQUEST_COUNT, KEY_VALUE_HEADS, WINDOW_LENGTH, HEAD_SIZE), 1.0, 6.0, ((0, 8), (1, 4)))
    rotated_sink_keys = normal_values(keys[6], (REQUEST_COUNT, KEY_VALUE_HEADS, SINK_POSITIONS, HEAD_SIZE), 1.5, 9.0, ((0, 8), (1, 4)))
    sink_value_rows = normal_values(keys[7], (REQUEST_COUNT, KEY_VALUE_HEADS, SINK_POSITIONS, HEAD_SIZE), 1.0, 6.0, ((0, 8), (1, 4)))
    slot_request = draw_slot_request(jax.random.fold_in(keys[16], 71), 0)
    cached_len = draw_cached_len(jax.random.fold_in(keys[16], 71), 0)
    new_count = uneven(keys[10], REQUEST_COUNT, REQUEST_COUNT * NEW_TOKEN_SLOTS * 3 // 4, NEW_TOKEN_SLOTS, 1).astype(jnp.int32)
    out_weight = normal_values(keys[11], (QUERY_HEADS * HEAD_SIZE, D), (QUERY_HEADS * HEAD_SIZE) ** -0.5, 0.0625, ((0, 4),))
    norm_gain = jnp.clip(1.0 + 0.1 * jax.random.normal(keys[12], (D,), jnp.float32), 0.5, 1.5).astype(jnp.bfloat16)
    gate_weight = normal_values(keys[13], (D, FF), D ** -0.5, 0.0625, ((0, 4), (1, 8)))
    up_weight = normal_values(keys[14], (D, FF), D ** -0.5, 0.0625, ((0, 4), (1, 8)))
    down_weight = normal_values(keys[15], (FF, D), FF ** -0.5, 0.0390625, ((0, 8), (1, 4)))
    return {"residual": residual, "queries": queries, "fresh_token_keys": fresh_token_keys, "fresh_token_values": fresh_token_values, "window_cache_keys": window_cache_keys, "window_cache_values": window_cache_values, "rotated_sink_keys": rotated_sink_keys, "sink_value_rows": sink_value_rows, "slot_request": slot_request, "cached_len": cached_len, "new_count": new_count, "out_weight": out_weight, "norm_gain": norm_gain, "gate_weight": gate_weight, "up_weight": up_weight, "down_weight": down_weight}


ROPE_THETA = 5000000.0
NORM_EPS = 1e-05
MASK_FILL = -1e+30

def rope_tables(positions, depth):
    half_depth = depth // 2
    exponent = 2.0 * jnp.arange(half_depth, dtype=jnp.float32) / depth
    frequency = jnp.exp(-jnp.log(jnp.float32(ROPE_THETA)) * exponent)
    angles = positions.astype(jnp.float32)[..., None] * frequency
    return (jnp.cos(angles), jnp.sin(angles))

def rotate(vectors, cosine, sine_table):
    half_depth = vectors.shape[-1] // 2
    front_half = vectors[..., :half_depth]
    back_half = vectors[..., half_depth:]
    return jnp.concatenate([front_half * cosine - back_half * sine_table, back_half * cosine + front_half * sine_table], axis=-1)

def reference(residual, queries, fresh_token_keys, fresh_token_values, window_cache_keys, window_cache_values, rotated_sink_keys, sink_value_rows, slot_request, cached_len, new_count, out_weight, norm_gain, gate_weight, up_weight, down_weight):
    query_heads_per_key = QUERY_HEADS // KEY_VALUE_HEADS
    scale = HEAD_SIZE ** (-0.5)
    lengths = cached_len[slot_request]
    counts = new_count[slot_request]
    query_all = queries.reshape(REQUEST_COUNT, NEW_TOKEN_SLOTS, QUERY_HEADS, HEAD_SIZE)
    joined_keys = fresh_token_keys.reshape(REQUEST_COUNT, NEW_TOKEN_SLOTS, KEY_VALUE_HEADS, HEAD_SIZE)
    joined_values = fresh_token_values.reshape(REQUEST_COUNT, NEW_TOKEN_SLOTS, KEY_VALUE_HEADS, HEAD_SIZE)

    def one_slot(packed):
        query_rows, key_rows, value_rows, window_keys, window_values, sink_krows, sink_vrows, length, count = packed
        token_ids = jnp.arange(NEW_TOKEN_SLOTS, dtype=jnp.int32)
        positions = length + token_ids
        cosine, sine_table = rope_tables(positions, HEAD_SIZE)
        rotated_query = rotate(query_rows.astype(jnp.float32), cosine[:, None], sine_table[:, None]).astype(jnp.bfloat16)
        k_rot = rotate(key_rows.astype(jnp.float32), cosine[:, None], sine_table[:, None]).astype(jnp.bfloat16)
        k_fresh = jnp.transpose(k_rot, (1, 0, 2))
        v_fresh = jnp.transpose(value_rows, (1, 0, 2))
        all_keys = jnp.concatenate([sink_krows, window_keys, k_fresh], axis=1)
        all_values = jnp.concatenate([sink_vrows, window_values, v_fresh], axis=1)
        slot_ids = jnp.arange(WINDOW_LENGTH, dtype=jnp.int32)
        held_pos = slot_ids + WINDOW_LENGTH * ((length - 1 - slot_ids) // WINDOW_LENGTH)
        slot_ok = (slot_ids < length) & (held_pos >= SINK_POSITIONS)
        window_ok = slot_ok[None, :] & (held_pos[None, :] > positions[:, None] - WINDOW_LENGTH)
        new_ok = (token_ids[None, :] < count) & (token_ids[None, :] <= token_ids[:, None])
        seen = jnp.concatenate([jnp.ones((NEW_TOKEN_SLOTS, SINK_POSITIONS), jnp.bool_), window_ok, new_ok], axis=1)
        grouped_heads = rotated_query.reshape(NEW_TOKEN_SLOTS, KEY_VALUE_HEADS, query_heads_per_key, HEAD_SIZE).astype(jnp.float32)
        scores = jnp.einsum('ikgd,ktd->kgit', grouped_heads, all_keys.astype(jnp.float32)) * scale
        scores = jnp.where(seen[None, None], scores, MASK_FILL)
        largest = lax.optimization_barrier(jnp.max(scores, axis=-1, keepdims=True))
        weights = jnp.exp(scores - largest)
        totals = lax.optimization_barrier(jnp.sum(weights, axis=-1))
        probs = weights.astype(jnp.bfloat16)
        context = jnp.einsum('kgit,ktd->ikgd', probs.astype(jnp.float32), all_values.astype(jnp.float32))
        context = context / jnp.transpose(totals, (2, 0, 1))[..., None]
        attended = context.astype(jnp.bfloat16).reshape(NEW_TOKEN_SLOTS, QUERY_HEADS * HEAD_SIZE)
        new_index = (slot_ids - length) % WINDOW_LENGTH
        written = new_index < count
        chosen = jnp.clip(new_index, 0, NEW_TOKEN_SLOTS - 1)
        keys_after = jnp.where(written[None, :, None], k_fresh[:, chosen], window_keys)
        values_after = jnp.where(written[None, :, None], v_fresh[:, chosen], window_values)
        return (attended, keys_after, values_after)
    attended, keys_after, values_after = lax.map(one_slot, (query_all, joined_keys, joined_values, window_cache_keys, window_cache_values, rotated_sink_keys, sink_value_rows, lengths, counts))
    flat = attended.reshape(TOKEN_SLOTS, QUERY_HEADS * HEAD_SIZE)
    stream = residual.astype(jnp.float32) + jnp.dot(flat, out_weight, preferred_element_type=jnp.float32)
    square = lax.optimization_barrier(jnp.mean(stream * stream, axis=1, keepdims=True))
    normed = (stream * lax.rsqrt(square + NORM_EPS) * norm_gain.astype(jnp.float32)).astype(jnp.bfloat16)
    col_width = D // N_TP
    gate_total = jnp.zeros((TOKEN_SLOTS, FF), jnp.float32)
    up_total = jnp.zeros((TOKEN_SLOTS, FF), jnp.float32)
    for shard_idx in range(N_TP):
        columns = normed[:, shard_idx * col_width:(shard_idx + 1) * col_width]
        gate_part = jnp.dot(columns, gate_weight[shard_idx * col_width:(shard_idx + 1) * col_width], preferred_element_type=jnp.float32).astype(jnp.bfloat16)
        up_part = jnp.dot(columns, up_weight[shard_idx * col_width:(shard_idx + 1) * col_width], preferred_element_type=jnp.float32).astype(jnp.bfloat16)
        gate_part, up_part = lax.optimization_barrier((gate_part, up_part))
        gate_total = gate_total + gate_part.astype(jnp.float32)
        up_total = up_total + up_part.astype(jnp.float32)
    hidden = (jax.nn.silu(gate_total) * up_total).astype(jnp.bfloat16)
    output_slots = (stream + jnp.dot(hidden, down_weight, preferred_element_type=jnp.float32)).astype(jnp.bfloat16)
    slot_of = jnp.argsort(slot_request).astype(jnp.int32)
    block_output = output_slots.reshape(REQUEST_COUNT, NEW_TOKEN_SLOTS, D)[slot_of].reshape(TOKEN_SLOTS, D)
    return (block_output, keys_after[slot_of], values_after[slot_of])
```

```python
import jax
import jax.numpy as jnp
from jax import lax
from jax.experimental import pallas as pl
from jax.experimental.pallas import tpu as pltpu
from jax.sharding import PartitionSpec as P

ROPE_THETA = 5000000.0
NORM_EPS = 1e-05
MASK_FILL = -1e30


def rope_tables(positions, depth):
    half_depth = depth // 2
    exponent = 2.0 * jnp.arange(half_depth, dtype=jnp.float32) / depth
    frequency = jnp.exp(-jnp.log(jnp.float32(ROPE_THETA)) * exponent)
    angles = positions.astype(jnp.float32)[..., None] * frequency
    return (jnp.cos(angles), jnp.sin(angles))


def rotate(vectors, cosine, sine_table):
    half_depth = vectors.shape[-1] // 2
    front_half = vectors[..., :half_depth]
    back_half = vectors[..., half_depth:]
    return jnp.concatenate(
        [
            front_half * cosine - back_half * sine_table,
            back_half * cosine + front_half * sine_table,
        ],
        axis=-1,
    )


SIBLING = [(t, t ^ 1) for t in range(4)]
ACROSS = [(t, t ^ 2) for t in range(4)]
ASIDE = [(g, g ^ 1) for g in range(8)]
UP = [(g, g + 2) for g in range(6)]
DOWN = [(g + 2, g) for g in range(6)]


def summed_with(mine, yours, partners):
    got = lax.ppermute(yours.astype(jnp.bfloat16), "tp", partners)
    return mine.astype(jnp.float32) + got.astype(jnp.float32)


def columns(parts, start, width):
    return jnp.concatenate(
        [lax.dynamic_slice_in_dim(part, start, width, 1) for part in parts], axis=1
    )


def side_by_side(value, bit, partners):
    got = lax.ppermute(value, "tp", partners)
    return jnp.concatenate(
        [jnp.where(bit == 0, value, got), jnp.where(bit == 0, got, value)], axis=1
    )


def patch_kernel(slot_ref, length_ref, count_ref, keys, values, new_keys, new_values, out):
    slot = slot_ref[pl.program_id(0)]
    window, depth = keys.shape[2:]
    new_rows = new_keys.shape[2]
    start, count = lax.rem(length_ref[slot], window), count_ref[slot]

    def since(width):
        rel = lax.broadcasted_iota(jnp.int32, (window, width), 0) - start
        return jnp.where(rel < 0, rel + window, rel)

    token = lax.broadcasted_iota(jnp.int32, (window, new_rows), 1)
    chosen = jnp.where(since(new_rows) == token, 1.0, 0.0).astype(jnp.bfloat16)
    written = since(depth) < count
    for which, (cache, fresh) in enumerate(((keys, new_keys), (values, new_values))):
        for head in range(keys.shape[1]):
            moved = jnp.dot(chosen, fresh[0, head], preferred_element_type=jnp.float32)
            held = cache[0, head].astype(jnp.float32)
            out[0, which, head] = jnp.where(written, moved, held).astype(jnp.bfloat16)


def updated_caches(send_slot, lengths, counts, keys, values, new_keys, new_values):
    groups = send_slot.shape[0]
    _, heads, window, depth = keys.shape
    new_rows = new_keys.shape[2]

    def by_slot(rows):
        return pl.BlockSpec((1, heads, rows, depth), lambda d, slot, *_: (slot[d], 0, 0, 0))

    return pl.pallas_call(
        patch_kernel,
        out_shape=jax.ShapeDtypeStruct((groups, 2, heads, window, depth), jnp.bfloat16),
        grid_spec=pltpu.PrefetchScalarGridSpec(
            num_scalar_prefetch=3,
            grid=(groups,),
            in_specs=[by_slot(window), by_slot(window), by_slot(new_rows), by_slot(new_rows)],
            out_specs=pl.BlockSpec(
                (1, 2, heads, window, depth), lambda d, *_: (d, 0, 0, 0, 0)
            ),
        ),
        compiler_params=pltpu.CompilerParams(vmem_limit_bytes=32 * 1024 * 1024),
        name="updated_caches",
    )(send_slot, lengths, counts, keys, values, new_keys, new_values)


def shards_any(
    residual,
    queries,
    fresh_token_keys,
    fresh_token_values,
    window_cache_keys,
    window_cache_values,
    rotated_sink_keys,
    sink_value_rows,
    slot_request,
    cached_len,
    new_count,
    out_weight,
    norm_gain,
    gate_weight,
    up_weight,
    down_weight,
):
    group_idx = lax.axis_index("req")
    tp_idx = lax.axis_index("tp")
    groups = lax.axis_size("req")
    held_reqs, kv_local, window, depth = window_cache_keys.shape
    sink_rows = rotated_sink_keys.shape[2]
    tok_dev = residual.shape[0]
    col_width = residual.shape[1]
    new_rows = tok_dev // held_reqs
    query_heads_per_key = queries.shape[1] // (kv_local * depth)
    total_reqs = slot_request.shape[0]
    scale = depth ** (-0.5)
    request_ids = jnp.arange(total_reqs, dtype=jnp.int32)
    my_requests = lax.dynamic_slice_in_dim(slot_request, group_idx * held_reqs, held_reqs)
    matches = my_requests[:, None] == request_ids[None, :]
    lengths = jnp.sum(jnp.where(matches, cached_len[None, :], 0), axis=1)
    counts = jnp.sum(jnp.where(matches, new_count[None, :], 0), axis=1)
    slot_of = jnp.sum(
        jnp.where(slot_request[None, :] == request_ids[:, None], request_ids[None, :], 0), axis=1
    )
    token_ids = jnp.arange(new_rows, dtype=jnp.int32)
    positions = lengths[:, None] + token_ids[None, :]
    cosine, sine_table = rope_tables(positions, depth)
    rotated_query = rotate(
        queries.reshape(held_reqs, new_rows, kv_local, query_heads_per_key, depth).astype(
            jnp.float32
        ),
        cosine[:, :, None, None],
        sine_table[:, :, None, None],
    ).astype(jnp.bfloat16)
    k_rot = rotate(
        fresh_token_keys.reshape(held_reqs, new_rows, kv_local, depth).astype(jnp.float32),
        cosine[:, :, None],
        sine_table[:, :, None],
    ).astype(jnp.bfloat16)
    k_fresh = jnp.transpose(k_rot, (0, 2, 1, 3))
    v_fresh = jnp.transpose(
        fresh_token_values.reshape(held_reqs, new_rows, kv_local, depth), (0, 2, 1, 3)
    )
    first_keys = jnp.concatenate([rotated_sink_keys, k_fresh], axis=2)
    first_values = jnp.concatenate([sink_value_rows, v_fresh], axis=2)
    new_ok = (token_ids[None, None, :] < counts[:, None, None]) & (
        token_ids[None, None, :] <= token_ids[None, :, None]
    )
    first_ok = jnp.concatenate(
        [jnp.ones((held_reqs, new_rows, sink_rows), jnp.bool_), new_ok], axis=2
    )
    scores = (
        jnp.einsum(
            "rikgd,rktd->rkigt", rotated_query, first_keys, preferred_element_type=jnp.float32
        )
        * scale
    )
    scores = jnp.where(first_ok[:, None, :, None, :], scores, MASK_FILL)
    running = jnp.max(scores, axis=-1, keepdims=True)
    weights = jnp.exp(scores - running)
    totals = jnp.sum(weights, axis=-1, keepdims=True)
    context = jnp.einsum(
        "rkigt,rktd->rkigd",
        weights.astype(jnp.bfloat16),
        first_values,
        preferred_element_type=jnp.float32,
    )
    key_span = min(256, window)
    live = jnp.minimum(lengths, window)
    blocks_needed = jnp.max((live + key_span - 1) // key_span)

    def key_block(block_idx, carry):
        run_max, run_total, run_context = carry
        start_slot = block_idx * key_span
        block_keys = lax.dynamic_slice_in_dim(window_cache_keys, start_slot, key_span, 2)
        block_values = lax.dynamic_slice_in_dim(window_cache_values, start_slot, key_span, 2)
        slot_ids = start_slot + jnp.arange(key_span, dtype=jnp.int32)
        held_pos = slot_ids[None, :] + window * (
            (lengths[:, None] - 1 - slot_ids[None, :]) // window
        )
        slot_ok = (slot_ids[None, :] < lengths[:, None]) & (held_pos >= sink_rows)
        block_ok = slot_ok[:, None, :] & (held_pos[:, None, :] > positions[:, :, None] - window)
        block_scores = (
            jnp.einsum(
                "rikgd,rktd->rkigt", rotated_query, block_keys, preferred_element_type=jnp.float32
            )
            * scale
        )
        block_scores = jnp.where(block_ok[:, None, :, None, :], block_scores, MASK_FILL)
        new_max = jnp.maximum(run_max, jnp.max(block_scores, axis=-1, keepdims=True))
        factor = jnp.exp(run_max - new_max)
        block_weights = jnp.exp(block_scores - new_max)
        run_total = run_total * factor + jnp.sum(block_weights, axis=-1, keepdims=True)
        run_context = run_context * factor + jnp.einsum(
            "rkigt,rktd->rkigd",
            block_weights.astype(jnp.bfloat16),
            block_values,
            preferred_element_type=jnp.float32,
        )
        return (new_max, run_total, run_context)

    running, totals, context = lax.fori_loop(
        0, blocks_needed, key_block, (running, totals, context)
    )
    attended = (context / totals).astype(jnp.bfloat16)
    attended = jnp.transpose(attended, (0, 2, 1, 3, 4)).reshape(tok_dev, queries.shape[1])
    partial_value = jnp.dot(attended, out_weight, preferred_element_type=jnp.float32)
    own_cols = lax.dynamic_slice_in_dim(
        partial_value, tp_idx * col_width, col_width, 1
    ) + residual.astype(jnp.float32)
    partial_value = lax.dynamic_update_slice_in_dim(partial_value, own_cols, tp_idx * col_width, 1)
    summed_rows = lax.psum(partial_value.astype(jnp.bfloat16), "tp").astype(jnp.float32)
    square = jnp.mean(summed_rows * summed_rows, axis=1, keepdims=True)
    stream = lax.dynamic_slice_in_dim(summed_rows, tp_idx * col_width, col_width, 1)
    normed = (stream * lax.rsqrt(square + NORM_EPS) * norm_gain.astype(jnp.float32)).astype(
        jnp.bfloat16
    )
    piece_rows = lax.all_gather(normed, "req", axis=0, tiled=True)
    gate_part = jnp.dot(piece_rows, gate_weight, preferred_element_type=jnp.float32)
    up_part = jnp.dot(piece_rows, up_weight, preferred_element_type=jnp.float32)
    paired = jnp.stack([gate_part, up_part], axis=1)
    summed = lax.psum(paired.astype(jnp.bfloat16), "tp").astype(jnp.float32)
    hidden = (jax.nn.silu(summed[:, 0]) * summed[:, 1]).astype(jnp.bfloat16)
    hidden_nat = jnp.take(
        hidden.reshape(total_reqs, new_rows, hidden.shape[1]), slot_of, axis=0
    ).reshape(total_reqs * new_rows, hidden.shape[1])
    placed = (
        jnp.zeros((total_reqs, new_rows, col_width), jnp.float32)
        .at[my_requests]
        .set(stream.reshape(held_reqs, new_rows, col_width))
    )
    placed = placed.reshape(total_reqs * new_rows, col_width)
    block_output = lax.psum_scatter(
        (jnp.dot(hidden_nat, down_weight, preferred_element_type=jnp.float32) + placed).astype(
            jnp.bfloat16
        ),
        "req",
        scatter_dimension=0,
        tiled=True,
    )
    slot_ids = jnp.arange(window, dtype=jnp.int32)
    new_index = (slot_ids[None, :] - lengths[:, None]) % window
    written = new_index < counts[:, None]
    one_hot = ((new_index[:, :, None] == token_ids[None, None, :]) & written[:, :, None]).astype(
        jnp.bfloat16
    )
    keys_moved = jnp.einsum(
        "rwj,rkjd->rkwd", one_hot, k_fresh, preferred_element_type=jnp.float32
    ).astype(jnp.bfloat16)
    values_moved = jnp.einsum(
        "rwj,rkjd->rkwd", one_hot, v_fresh, preferred_element_type=jnp.float32
    ).astype(jnp.bfloat16)
    keys_after = jnp.where(written[:, None, :, None], keys_moved, window_cache_keys)
    values_after = jnp.where(written[:, None, :, None], values_moved, window_cache_values)
    dest_dev = my_requests // held_reqs
    send_keys = (
        jnp.zeros((groups,) + window_cache_keys.shape[1:], jnp.bfloat16)
        .at[dest_dev]
        .set(keys_after)
    )
    send_values = (
        jnp.zeros((groups,) + window_cache_values.shape[1:], jnp.bfloat16)
        .at[dest_dev]
        .set(values_after)
    )
    got_keys, got_values = (
        lax.all_to_all(send_keys, "req", split_axis=0, concat_axis=0, tiled=True),
        lax.all_to_all(send_values, "req", split_axis=0, concat_axis=0, tiled=True),
    )
    source_group = lax.dynamic_slice_in_dim(slot_of, group_idx * held_reqs, held_reqs) // held_reqs
    decode_keys = jnp.take(got_keys, source_group, axis=0)
    decode_values = jnp.take(got_values, source_group, axis=0)
    return (block_output, decode_keys, decode_values)


def shards_line(
    residual,
    queries,
    fresh_token_keys,
    fresh_token_values,
    window_cache_keys,
    window_cache_values,
    rotated_sink_keys,
    sink_value_rows,
    slot_request,
    cached_len,
    new_count,
    out_weight,
    norm_gain,
    gate_weight,
    up_weight,
    down_weight,
):
    group_idx = lax.axis_index("req")
    tp_idx = lax.axis_index("tp")
    groups = lax.axis_size("req")
    held_reqs, kv_local, window, depth = window_cache_keys.shape
    sink_rows = rotated_sink_keys.shape[2]
    tok_dev = residual.shape[0]
    col_width = residual.shape[1]
    new_rows = tok_dev // held_reqs
    query_heads_per_key = queries.shape[1] // (kv_local * depth)
    total_reqs = slot_request.shape[0]
    z_idx, x_idx = group_idx // 2, group_idx % 2
    scale = depth ** (-0.5)
    request_ids = jnp.arange(total_reqs, dtype=jnp.int32)
    my_requests = lax.dynamic_slice_in_dim(slot_request, group_idx * held_reqs, held_reqs)
    matches = my_requests[:, None] == request_ids[None, :]
    lengths = jnp.sum(jnp.where(matches, cached_len[None, :], 0), axis=1)
    counts = jnp.sum(jnp.where(matches, new_count[None, :], 0), axis=1)
    slot_of = jnp.sum(
        jnp.where(slot_request[None, :] == request_ids[:, None], request_ids[None, :], 0), axis=1
    )
    token_ids = jnp.arange(new_rows, dtype=jnp.int32)
    positions = lengths[:, None] + token_ids[None, :]
    cosine, sine_table = rope_tables(positions, depth)
    rotated_query = rotate(
        queries.reshape(held_reqs, new_rows, kv_local, query_heads_per_key, depth).astype(
            jnp.float32
        ),
        cosine[:, :, None, None],
        sine_table[:, :, None, None],
    ).astype(jnp.bfloat16)
    k_rot = rotate(
        fresh_token_keys.reshape(held_reqs, new_rows, kv_local, depth).astype(jnp.float32),
        cosine[:, :, None],
        sine_table[:, :, None],
    ).astype(jnp.bfloat16)
    k_fresh = jnp.transpose(k_rot, (0, 2, 1, 3))
    v_fresh = jnp.transpose(
        fresh_token_values.reshape(held_reqs, new_rows, kv_local, depth), (0, 2, 1, 3)
    )
    my_dest = my_requests // held_reqs
    send_slot = jnp.sum(
        jnp.where(
            my_dest[None, :] == jnp.arange(groups, dtype=jnp.int32)[:, None],
            jnp.arange(held_reqs, dtype=jnp.int32)[None, :],
            0,
        ),
        axis=1,
    )
    first_keys = jnp.concatenate([rotated_sink_keys, k_fresh], axis=2)
    first_values = jnp.concatenate([sink_value_rows, v_fresh], axis=2)
    new_ok = (token_ids[None, None, :] < counts[:, None, None]) & (
        token_ids[None, None, :] <= token_ids[None, :, None]
    )
    first_ok = jnp.concatenate(
        [jnp.ones((held_reqs, new_rows, sink_rows), jnp.bool_), new_ok], axis=2
    )
    scores = (
        jnp.einsum(
            "rikgd,rktd->rkigt", rotated_query, first_keys, preferred_element_type=jnp.float32
        )
        * scale
    )
    scores = jnp.where(first_ok[:, None, :, None, :], scores, MASK_FILL)
    running = jnp.max(scores, axis=-1, keepdims=True)
    weights = jnp.exp(scores - running)
    totals = jnp.sum(weights, axis=-1, keepdims=True)
    context = jnp.einsum(
        "rkigt,rktd->rkigd",
        weights.astype(jnp.bfloat16),
        first_values,
        preferred_element_type=jnp.float32,
    )
    key_span = min(256, window)
    live = jnp.minimum(lengths, window)
    blocks_needed = jnp.max((live + key_span - 1) // key_span)

    def key_block(block_idx, carry):
        run_max, run_total, run_context = carry
        start_slot = block_idx * key_span
        block_keys = lax.dynamic_slice_in_dim(window_cache_keys, start_slot, key_span, 2)
        block_values = lax.dynamic_slice_in_dim(window_cache_values, start_slot, key_span, 2)
        slot_ids = start_slot + jnp.arange(key_span, dtype=jnp.int32)
        held_pos = slot_ids[None, :] + window * (
            (lengths[:, None] - 1 - slot_ids[None, :]) // window
        )
        slot_ok = (slot_ids[None, :] < lengths[:, None]) & (held_pos >= sink_rows)
        block_ok = slot_ok[:, None, :] & (held_pos[:, None, :] > positions[:, :, None] - window)
        block_scores = (
            jnp.einsum(
                "rikgd,rktd->rkigt", rotated_query, block_keys, preferred_element_type=jnp.float32
            )
            * scale
        )
        block_scores = jnp.where(block_ok[:, None, :, None, :], block_scores, MASK_FILL)
        new_max = jnp.maximum(run_max, jnp.max(block_scores, axis=-1, keepdims=True))
        factor = jnp.exp(run_max - new_max)
        block_weights = jnp.exp(block_scores - new_max)
        run_total = run_total * factor + jnp.sum(block_weights, axis=-1, keepdims=True)
        run_context = run_context * factor + jnp.einsum(
            "rkigt,rktd->rkigd",
            block_weights.astype(jnp.bfloat16),
            block_values,
            preferred_element_type=jnp.float32,
        )
        return (new_max, run_total, run_context)

    running, totals, context = lax.fori_loop(
        0, blocks_needed, key_block, (running, totals, context)
    )
    attended = (context / totals).astype(jnp.bfloat16)
    attended = jnp.transpose(attended, (0, 2, 1, 3, 4)).reshape(tok_dev, queries.shape[1])
    core, y_idx = tp_idx % 2, tp_idx // 2
    partial_value = jnp.dot(attended, out_weight, preferred_element_type=jnp.float32)
    partial_value = partial_value.astype(jnp.bfloat16)
    halves = (partial_value[:, : 2 * col_width], partial_value[:, 2 * col_width :])
    stream = summed_with(
        columns(halves, core * col_width, col_width),
        columns(halves, (1 - core) * col_width, col_width),
        SIBLING,
    )
    stream = summed_with(
        columns((stream,), y_idx * col_width, col_width),
        columns((stream,), (1 - y_idx) * col_width, col_width),
        ACROSS,
    )
    stream = stream + residual.astype(jnp.float32)
    square = jnp.sum(stream * stream, axis=1, keepdims=True)
    square = square + lax.ppermute(square, "tp", SIBLING)
    square = (square + lax.ppermute(square, "tp", ACROSS)) / (col_width * 4)
    normed = (stream * lax.rsqrt(square + NORM_EPS) * norm_gain.astype(jnp.float32)).astype(
        jnp.bfloat16
    )
    up_1, down_1 = lax.ppermute(normed, "req", UP), lax.ppermute(normed, "req", DOWN)
    piece_1 = jnp.where(z_idx < 2, down_1, up_1)
    up_2, down_2 = lax.ppermute(up_1, "req", UP), lax.ppermute(down_1, "req", DOWN)
    piece_2 = jnp.where(z_idx < 2, down_2, up_2)
    up_3, down_3 = lax.ppermute(up_2, "req", UP), lax.ppermute(down_2, "req", DOWN)
    piece_3 = jnp.where(
        z_idx == 0, down_3, jnp.where(z_idx == 1, up_1, jnp.where(z_idx == 2, down_1, up_3))
    )
    ff = gate_weight.shape[1]
    whole = [
        jnp.concatenate([piece, lax.ppermute(piece, "req", ASIDE)], axis=0)
        for piece in (normed, piece_1, piece_2, piece_3)
    ]
    whole[2:], (send_keys, send_values) = lax.optimization_barrier(
        (whole[2:], (k_fresh, v_fresh))
    )
    outgoing = updated_caches(
        send_slot, lengths, counts, window_cache_keys, window_cache_values, send_keys, send_values
    )
    arrived = lax.all_to_all(outgoing, "req", split_axis=0, concat_axis=0, tiled=True)
    products = []
    for chunk in range(2):
        rows = jnp.concatenate(whole[2 * chunk : 2 * chunk + 2], axis=0)
        parts = [
            jnp.dot(rows, weight, preferred_element_type=jnp.float32).astype(jnp.bfloat16)
            for weight in (gate_weight, up_weight)
        ]
        summed = summed_with(
            columns(parts, core * (ff // 2), ff // 2),
            columns(parts, (1 - core) * (ff // 2), ff // 2),
            SIBLING,
        )
        parts = (summed[:, : ff // 2], summed[:, ff // 2 :])
        summed = summed_with(
            columns(parts, y_idx * (ff // 4), ff // 4),
            columns(parts, (1 - y_idx) * (ff // 4), ff // 4),
            ACROSS,
        )
        hidden = (jax.nn.silu(summed[:, : ff // 4]) * summed[:, ff // 4 :]).astype(jnp.bfloat16)
        hidden = side_by_side(side_by_side(hidden, y_idx, ACROSS), core, SIBLING)
        product = jnp.dot(hidden, down_weight, preferred_element_type=jnp.float32)
        if chunk == 0:
            product = product + jnp.pad(stream, ((0, product.shape[0] - tok_dev), (0, 0)))
        products.append(product.astype(jnp.bfloat16))
    z_order = jnp.asarray(
        [[0, 1, 2, 3], [1, 2, 3, 0], [2, 1, 0, 3], [3, 2, 1, 0]], jnp.int32
    )[z_idx]
    held_groups = (
        z_order[:, None] * 2 + (x_idx ^ jnp.arange(2, dtype=jnp.int32))[None, :]
    ).reshape(groups)
    place = jnp.sum(
        jnp.where(
            held_groups[None, :] == (slot_of // held_reqs)[:, None],
            jnp.arange(groups, dtype=jnp.int32)[None, :],
            0,
        ),
        axis=1,
    )
    rows_of = (place * held_reqs + slot_of % held_reqs).reshape(groups // 2, 2, held_reqs)
    slabs = jnp.concatenate(products, axis=0).reshape(total_reqs, new_rows, col_width)

    def rows_for(z_pair, x_dest):
        wanted = lax.dynamic_index_in_dim(rows_of, x_dest, 1, keepdims=False)
        wanted = jnp.concatenate([wanted[z] for z in z_pair])
        return jnp.take(slabs, wanted, axis=0).reshape(2, tok_dev, col_width)

    pairs = []
    for z_pair in ((0, 3), (1, 2)):
        got = lax.ppermute(rows_for(z_pair, 1 - x_idx), "req", ASIDE)
        pairs.append(rows_for(z_pair, x_idx).astype(jnp.float32) + got.astype(jnp.float32))

    def for_z(dest):
        low = jnp.where(dest <= 0, pairs[0][0], pairs[0][1])
        mid = jnp.where(dest == 1, pairs[1][0], pairs[1][1])
        return jnp.where((dest == 1) | (dest == 2), mid, low)

    rising, falling = lax.ppermute(pairs[0][1].astype(jnp.bfloat16), "req", UP), lax.ppermute(
        pairs[0][0].astype(jnp.bfloat16), "req", DOWN
    )
    for step in (2, 3):
        rise = for_z(z_idx + 4 - step) + rising.astype(jnp.float32)
        fall = for_z(z_idx - 4 + step) + falling.astype(jnp.float32)
        rising = lax.ppermute(rise.astype(jnp.bfloat16), "req", UP)
        falling = lax.ppermute(fall.astype(jnp.bfloat16), "req", DOWN)
    block_output = (
        for_z(z_idx) + rising.astype(jnp.float32) + falling.astype(jnp.float32)
    ).astype(jnp.bfloat16)
    source_group = lax.dynamic_slice_in_dim(slot_of, group_idx * held_reqs, held_reqs) // held_reqs
    decode_keys = jnp.take(arrived[:, 0], source_group, axis=0)
    decode_values = jnp.take(arrived[:, 1], source_group, axis=0)
    return (block_output, decode_keys, decode_values)


def solution(mesh):
    placed = (
        P("req", "tp"),
        P("req", "tp"),
        P("req", "tp"),
        P("req", "tp"),
        P("req", "tp", None, None),
        P("req", "tp", None, None),
        P("req", "tp", None, None),
        P("req", "tp", None, None),
        P(),
        P(),
        P(),
        P("tp", None),
        P("tp"),
        P("tp", "req"),
        P("tp", "req"),
        P("req", "tp"),
    )
    line = mesh.shape["req"] == 8 and mesh.shape["tp"] == 4
    return jax.shard_map(
        shards_line if line else shards_any,
        mesh=mesh,
        in_specs=placed,
        out_specs=(P("req", "tp"), P("req", "tp", None, None), P("req", "tp", None, None)),
        check_vma=False,
    )
```
